256 devices in a mesh: grp: 2 (over core), row: 16 (over x_lo, z), col: 8 (over y, x_hi).
Axes of the slice: x: 4 (x_hi: 2, x_lo: 2; x = x_hi * 2 + x_lo), y: 4, z: 8, core: 2. Of those that a mesh axis runs over, the one named last changes fastest.
Arguments:
- occ_orbitals: float32 [32, 128, 128, 128], P(('grp', 'col'), 'row'), may hold values from -12 to 12
- vir_orbitals: float32 [256, 128, 128, 128], P(('grp', 'col'), 'row'), may hold values from -12 to 12
- xc_kernel: float32 [128, 128, 128], P('row'), may hold values from -8 to 0
- pairs: int32 [256, 2], P(('grp', 'col')), may hold values from 0 to 255, as said below
- batch_slot: int32 [16], replicated, may hold values from 0 to 15
Outputs:
- coupling: float32 [256, 16], P(('grp', 'col'))
The draws below stay inside these ranges and needn't reach their ends.
Inputs may be any that keep to these rules, and one draw needn't show every extreme that they name: `pairs`: column 0 is an occupied orbital below 32 and column 1 a virtual orbital; the virtual orbitals of rows b * 16 to (b + 1) * 16 - 1 lie in b * 16 to (b + 1) * 16 - 1; no pair appears twice.
All inputs are finite; a program needn't handle non-finite values.
Results may differ from the reference program's by a relative error of at most 0.00005.
Values sent between devices are 32-bit elements; how exact they have to be, the bound alone decides.
No kernel may reach another device: no remote copies, remote signals or barrier semaphores. Data moves between devices by JAX's collectives and lax.ppermute only.
A program may use at most 128 MiB of HBM per device.

```python
import math
import jax
import jax.numpy as jnp
from jax import lax

GRID = 128
NOCC = 32
NVIR = 256
PAIR_BLK = 16
BLOCKS = 16
VIR_LOC = 16
NPAIR = 256


def bump_factors(centers, alpha):
    grid_pos = jnp.arange(GRID, dtype=jnp.float32)
    return jnp.exp(alpha * (jnp.cos((grid_pos - centers[..., None]) * (2.0 * math.pi / GRID)) - 1.0))


def bump_field(key, number, alpha, low, high, scale):
    sub_keys = jax.random.split(key, 3)
    centers = jax.random.uniform(sub_keys[0], (number, 2, 3), jnp.float32) * GRID
    sign_values = jnp.where(jax.random.bernoulli(sub_keys[1], 0.5, (number, 2)), 1.0, -1.0)
    weights = sign_values * jnp.array([1.0, 0.6], jnp.float32)
    factor = bump_factors(centers, alpha)
    envelope = weights[:, 0, None, None, None] * factor[:, 0, 0, :, None, None] * factor[:, 0, 1, None, :, None] * factor[:, 0, 2, None, None, :]
    envelope = envelope + weights[:, 1, None, None, None] * factor[:, 1, 0, :, None, None] * factor[:, 1, 1, None, :, None] * factor[:, 1, 2, None, None, :]
    roughness = jax.random.uniform(sub_keys[2], (number, GRID, GRID, GRID), jnp.float32, low, high)
    return (scale * envelope * roughness).astype(jnp.float32)


def draw_occ_orbitals(key, part):
    key = jax.random.fold_in(key, 11)
    return bump_field(key, NOCC, 1.0, 0.5, 1.5, 4.8)


def draw_vir_orbitals(key, part):
    key = jax.random.fold_in(key, 12)
    return bump_field(key, NVIR, 1.0, 0.5, 1.5, 4.8)


def kernel_field(key, base, low, high):
    center_key, rough_key = jax.random.split(key)
    centers = jax.random.uniform(center_key, (3, 3), jnp.float32) * GRID
    factor = bump_factors(centers, 2.0)
    bumps = jnp.sum(factor[:, 0, :, None, None] * factor[:, 1, None, :, None] * factor[:, 2, None, None, :], axis=0)
    roughness = jax.random.uniform(rough_key, (GRID, GRID, GRID), jnp.float32, low, high)
    return (-(base + 1.5 * bumps) * roughness).astype(jnp.float32)


def draw_xc_kernel(key, part):
    key = jax.random.fold_in(key, 13)
    return kernel_field(key, 0.3, 0.6, 1.4)


def draw_pairs(key, part):
    key = jax.random.fold_in(key, 14)
    combos = NOCC * VIR_LOC
    block_keys = jax.random.split(key, BLOCKS)

    def one_block(block_key, block_index):
        perm_key, place_key = jax.random.split(block_key)
        shuffled = jax.random.permutation(perm_key, combos).astype(jnp.int32)
        located = jnp.argmax(shuffled == combos - 1).astype(jnp.int32)
        placed = jax.random.randint(place_key, (), 0, PAIR_BLK, dtype=jnp.int32)
        shuffled = jnp.roll(shuffled, placed - located)
        picked = shuffled[:PAIR_BLK]
        return jnp.stack([picked // VIR_LOC, block_index * VIR_LOC + picked % VIR_LOC], axis=1)
    blocks = jax.vmap(one_block)(block_keys, jnp.arange(BLOCKS, dtype=jnp.int32))
    return blocks.reshape(BLOCKS * PAIR_BLK, 2).astype(jnp.int32)


def set_ends(values, stream_key, smallest, largest):
    spot = [jax.random.randint(jax.random.fold_in(stream_key, axis), (), 0, length) for axis, length in enumerate(values.shape)]
    longest = values.shape.index(max(values.shape))
    beside = spot[:longest] + [(spot[longest] + 1) % values.shape[longest]] + spot[longest + 1:]
    return values.at[tuple(spot)].set(smallest).at[tuple(beside)].set(largest)


def setup_inputs(seed: int = 0) -> dict:
    key_list = jax.random.split(jax.random.key(seed), 6)
    occ_orbitals = draw_occ_orbitals(jax.random.fold_in(key_list[5], 71), 0)
    vir_orbitals = draw_vir_orbitals(jax.random.fold_in(key_list[5], 71), 0)
    xc_kernel = draw_xc_kernel(jax.random.fold_in(key_list[5], 71), 0)
    pairs = draw_pairs(jax.random.fold_in(key_list[5], 71), 0)
    batch_slot = set_ends(jax.random.randint(key_list[4], (BLOCKS,), 0, PAIR_BLK), jax.random.fold_in(key_list[4], 1), 0, PAIR_BLK - 1).astype(jnp.int32)
    return dict(occ_orbitals=occ_orbitals, vir_orbitals=vir_orbitals, xc_kernel=xc_kernel, pairs=pairs, batch_slot=batch_slot)


COULOMB = 0.4


def coulomb_kernel():
    frequency = jnp.arange(GRID, dtype=jnp.int32)
    signed = ((frequency + GRID // 2) % GRID - GRID // 2).astype(jnp.float32)
    square = signed * signed
    squared_sum = square[:, None, None] + square[None, :, None] + square[None, None, :]
    return jnp.where(squared_sum > 0, COULOMB / jnp.maximum(squared_sum, 1.0), 0.0).astype(jnp.float32)


def reference(occ_orbitals, vir_orbitals, xc_kernel, pairs, batch_slot):
    kernel = coulomb_kernel()
    occ_index = pairs[:, 0].astype(jnp.int32)
    vir_index = pairs[:, 1].astype(jnp.int32)
    chosen = jnp.arange(BLOCKS, dtype=jnp.int32) * PAIR_BLK + batch_slot.astype(jnp.int32)
    sigma = occ_orbitals[occ_index[chosen]] * vir_orbitals[vir_index[chosen]]

    def hartree(density):
        spectrum = jnp.fft.fftn(density)
        return jnp.real(jnp.fft.ifftn(spectrum * kernel)).astype(density.dtype)

    hartree_field = lax.map(hartree, sigma)
    potential = (hartree_field + xc_kernel * sigma).reshape(BLOCKS, GRID * GRID * GRID)

    def block_rows(first_row):
        row_ids = first_row + jnp.arange(PAIR_BLK, dtype=jnp.int32)
        pair_density = occ_orbitals[occ_index[row_ids]] * vir_orbitals[vir_index[row_ids]]
        pair_density = pair_density.reshape(PAIR_BLK, GRID * GRID * GRID)
        product = lax.dot_general(pair_density, potential, (((1,), (1,)), ((), ())), precision=lax.Precision.HIGHEST)
        return product / float(GRID * GRID * GRID)

    coupling = lax.map(block_rows, jnp.arange(BLOCKS, dtype=jnp.int32) * PAIR_BLK)
    return coupling.reshape(NPAIR, BLOCKS)
```

```python
import jax
import jax.numpy as jnp
from jax import lax
from jax.experimental import pallas as pl
from jax.experimental.pallas import tpu as pltpu
from jax.sharding import PartitionSpec as P

COULOMB = 0.4
LANES = 128
BLOCK_AXES = ("grp", "col")
VMEM_BYTES = 48 * 1024 * 1024


def cas_table(length):
    indices = jnp.arange(length, dtype=jnp.int32)
    products = indices[:, None] * indices[None, :] % length
    angles = products.astype(jnp.float32) * (2.0 * jnp.pi / length)
    return jnp.cos(angles) + jnp.sin(angles)


def signed_square(frequency, length):
    signed = ((frequency + length // 2) % length - length // 2).astype(jnp.float32)
    return signed * signed


def hartree(density):
    planes, length, depth = density.shape
    cas_rows = cas_table(length)
    highest = lax.Precision.HIGHEST
    grid_field = jnp.dot(density, cas_rows, precision=highest)
    grid_field = jnp.einsum("xyz,yv->xvz", grid_field, cas_rows, precision=highest)
    columns = lax.all_to_all(grid_field, "row", split_axis=1, concat_axis=0, tiled=True)
    columns = jnp.einsum("xyz,xu->uyz", columns, cas_rows, precision=highest)
    y_width = columns.shape[1]
    frequency = jnp.arange(length, dtype=jnp.int32)
    local_y = lax.axis_index("row") * y_width + jnp.arange(y_width, dtype=jnp.int32)
    squared_sum = (
        signed_square(frequency, length)[:, None, None]
        + signed_square(local_y, length)[None, :, None]
        + signed_square(frequency, length)[None, None, :]
    )
    kernel = jnp.where(squared_sum > 0, COULOMB / jnp.maximum(squared_sum, 1.0), 0.0)
    columns = jnp.einsum("xyz,xu->uyz", columns * kernel, cas_rows, precision=highest)
    grid_field = lax.all_to_all(columns, "row", split_axis=0, concat_axis=1, tiled=True)
    grid_field = jnp.einsum("xyz,yv->xvz", grid_field, cas_rows, precision=highest)
    grid_field = jnp.dot(grid_field, cas_rows, precision=highest)
    return grid_field * (1.0 / float(length) ** 3)


RING_Y, RING_X = 4, 2


def shift_col(value, dy, dx):
    pairs = [
        (y * RING_X + x, (y + dy) % RING_Y * RING_X + (x + dx) % RING_X)
        for y in range(RING_Y)
        for x in range(RING_X)
    ]
    return lax.ppermute(value, "col", pairs)


OFFSETS = ((0, 0), (1, 0), (3, 0), (0, 1), (2, 0), (1, 1), (3, 1), (2, 1))


def spread(piece):
    half = piece.shape[0] // 2
    from_below = shift_col(piece, 1, 0)
    from_above = shift_col(piece, -1, 0)
    from_side = shift_col(piece, 0, 1)
    far_low = shift_col(from_below[:half], 1, 0)
    far_high = shift_col(from_above[half:], -1, 0)
    side_below = shift_col(from_side, 1, 0)
    side_above = shift_col(from_side, -1, 0)
    far = jnp.concatenate([far_low, far_high], axis=0)
    side_far = shift_col(far, 0, 1)
    return [piece, from_below, from_above, from_side, far, side_below, side_above, side_far]


def swap_core(value):
    return lax.ppermute(value, "grp", [(0, 1), (1, 0)])


def pick_kernel(index_ref, held_ref, out_ref):
    rows = out_ref.shape[1]
    for block in range(out_ref.shape[0]):
        index = index_ref[block]
        start = pl.multiple_of(index % 2 * rows, rows)
        out_ref[block] = held_ref[index // 2, pl.ds(start, rows), :]


def pick(held, index, rows):
    return pl.pallas_call(
        pick_kernel,
        out_shape=jax.ShapeDtypeStruct((index.shape[0], rows, LANES), jnp.float32),
        in_specs=[
            pl.BlockSpec(memory_space=pltpu.SMEM),
            pl.BlockSpec(memory_space=pltpu.VMEM),
        ],
        out_specs=pl.BlockSpec(memory_space=pltpu.VMEM),
        compiler_params=pltpu.CompilerParams(vmem_limit_bytes=VMEM_BYTES),
        name="pick_occ",
    )(index, held)


def density_kernel(occ_ref, vir_index_ref, place_ref, *refs):
    pieces, vir_ref, out_ref = refs[:8], refs[8], refs[9]
    index = occ_ref[pl.program_id(0)]
    rows = pieces[0].shape[1] // 2
    start = pl.multiple_of(index % 2 * rows, rows)
    for number, piece in enumerate(pieces):
        cells = pl.ds(pl.multiple_of(place_ref[number] * rows, rows), rows)
        out_ref[0, cells, :] = piece[index // 2, pl.ds(start, rows), :] * vir_ref[0, 0, cells, :]


def form_densities(occ_index, vir_index, place, pieces, vir):
    number = occ_index.shape[0]
    rows = vir.shape[2]
    whole = pl.BlockSpec(memory_space=pltpu.VMEM)
    return pl.pallas_call(
        density_kernel,
        grid_spec=pltpu.PrefetchScalarGridSpec(
            num_scalar_prefetch=3,
            grid=(number,),
            in_specs=[whole] * 8
            + [pl.BlockSpec((1, 1, rows, LANES), lambda p, occ, vir, place: (vir[p], place[8], 0, 0))],
            out_specs=pl.BlockSpec((1, rows, LANES), lambda p, occ, vir, place: (p, 0, 0)),
        ),
        out_shape=jax.ShapeDtypeStruct((number, rows, LANES), jnp.float32),
        compiler_params=pltpu.CompilerParams(vmem_limit_bytes=VMEM_BYTES),
        cost_estimate=pl.CostEstimate(
            flops=number * rows * LANES, bytes_accessed=16 * 1024 * 1024, transcendentals=0
        ),
        name="form_densities",
    )(occ_index, vir_index, place, *pieces, vir)


PAIR_GROUP = 4


def contract_kernel(own_ref, mate_ref, *refs):
    fields, out_ref, total = refs[:4], refs[4], refs[5]
    step = pl.program_id(0)
    rows = own_ref.shape[1]
    per_half = own_ref.shape[0]

    @pl.when(step == 0)
    def _():
        total[...] = jnp.zeros_like(total)

    for half, densities in enumerate((own_ref, mate_ref)):

        @pl.loop(0, per_half // PAIR_GROUP)
        def _(group):
            first = group * PAIR_GROUP
            sums = [None] * (PAIR_GROUP * 8)
            for tile in range(rows // 8):
                cells = pl.ds(tile * 8, 8)
                left = [densities[first + k, cells, :] for k in range(PAIR_GROUP)]
                right = [field[j, cells, :] for field in fields for j in range(2)]
                for k in range(PAIR_GROUP):
                    for b in range(8):
                        term = left[k] * right[b]
                        slot = k * 8 + b
                        sums[slot] = term if sums[slot] is None else sums[slot] + term
            base = (half * per_half + first) * 8
            for slot, value in enumerate(sums):
                total[base + slot] += value

    @pl.when(step == pl.num_programs(0) - 1)
    def _():
        lanes = jnp.sum(total[...], axis=1)
        out_ref[...] = lax.dot_general(
            jnp.ones((8, LANES), jnp.float32),
            lanes,
            (((1,), (1,)), ((), ())),
            precision=lax.Precision.HIGHEST,
            preferred_element_type=jnp.float32,
        )


def contract(own, mate, fields):
    pairs, rows, _ = own.shape
    tile = 64
    return pl.pallas_call(
        contract_kernel,
        grid=(rows // tile,),
        in_specs=[pl.BlockSpec((pairs, tile, LANES), lambda i: (0, i, 0))] * 2
        + [pl.BlockSpec((2, tile, LANES), lambda i: (0, i, 0))] * 4,
        out_specs=pl.BlockSpec((8, 2 * pairs * 8), lambda i: (0, 0)),
        out_shape=jax.ShapeDtypeStruct((8, 2 * pairs * 8), jnp.float32),
        scratch_shapes=[pltpu.VMEM((2 * pairs * 8, 8, LANES), jnp.float32)],
        compiler_params=pltpu.CompilerParams(vmem_limit_bytes=VMEM_BYTES),
        cost_estimate=pl.CostEstimate(
            flops=2 * 16 * pairs * rows * LANES, bytes_accessed=12 * 1024 * 1024, transcendentals=0
        ),
        name="contract",
    )(own, mate, *fields)


def on_device(occ_orbitals, vir_orbitals, xc_kernel, pairs, batch_slot):
    planes, size_y, size_z = xc_kernel.shape
    cell_count = planes * size_y * size_z
    row_count = lax.axis_size("row")
    scale = 1.0 / float(cell_count * row_count)
    grp = lax.axis_index("grp")
    col = lax.axis_index("col")
    blocks = lax.axis_size(BLOCK_AXES)
    block_index = grp * lax.axis_size("col") + col
    occ_local, vir_local = occ_orbitals.shape[0], vir_orbitals.shape[0]
    chunk_rows = cell_count // blocks // LANES
    half_rows = cell_count // 2 // LANES

    mate_pairs = swap_core(pairs)
    vir_halves = vir_orbitals.reshape(vir_local, 2, half_rows, LANES)
    mate_vir = swap_core(lax.dynamic_index_in_dim(vir_halves, 1 - grp, 1, keepdims=True))

    own_slot = jnp.take(batch_slot, block_index)
    own_pair = lax.dynamic_index_in_dim(pairs, own_slot, 0, keepdims=False)
    wanted = own_pair[0].astype(jnp.float32)
    chunks = occ_orbitals.reshape(occ_local, blocks, chunk_rows, LANES)
    chunks = chunks.transpose(1, 0, 2, 3).reshape(blocks, occ_local * chunk_rows, LANES)
    note = jnp.full((blocks, 8, LANES), wanted, jnp.float32)
    held = lax.all_to_all(
        jnp.concatenate([chunks, note], axis=1), BLOCK_AXES, 0, 0, tiled=True
    )
    wanted_all = held[:, occ_local * chunk_rows, 0].astype(jnp.int32)
    picked = pick(held, wanted_all, chunk_rows)
    own_occ = lax.all_to_all(picked, BLOCK_AXES, 0, 0, tiled=True)
    own_vir = lax.dynamic_index_in_dim(
        vir_orbitals, own_pair[1] - block_index * vir_local, 0, keepdims=False
    )
    sigma = own_occ.reshape(planes, size_y, size_z) * own_vir

    occ_pieces = spread(held[:, : occ_local * chunk_rows])

    potential = hartree(sigma) + xc_kernel * sigma
    halves = potential.reshape(2, half_rows, LANES)
    kept = lax.dynamic_index_in_dim(halves, grp, 0, keepdims=True)
    moved = swap_core(lax.dynamic_index_in_dim(halves, 1 - grp, 0, keepdims=True))
    fields = spread(jnp.concatenate([kept, moved], axis=0))

    own_y, own_x = col // RING_X, col % RING_X
    places = [
        (own_y + RING_Y - dy) % RING_Y * RING_X + (own_x + RING_X - dx) % RING_X
        for dy, dx in OFFSETS
    ]
    place = jnp.stack(places).astype(jnp.int32)
    zero = jnp.zeros((1,), jnp.int32)
    mate_block = (1 - grp) * lax.axis_size("col") + col
    own = form_densities(
        pairs[:, 0],
        pairs[:, 1] - block_index * vir_local,
        jnp.concatenate([place, zero + grp]),
        occ_pieces,
        vir_halves,
    )
    mate = form_densities(
        mate_pairs[:, 0],
        mate_pairs[:, 1] - mate_block * vir_local,
        jnp.concatenate([place, zero]),
        occ_pieces,
        mate_vir,
    )
    near = contract(own, mate, fields[:4])
    far = contract(own, mate, fields[4:])

    pair_count = pairs.shape[0]
    sums = jnp.stack([near[0], far[0]]).reshape(2, 2, pair_count * 8)
    sums = sums.transpose(1, 0, 2)
    sums = jnp.where(grp == 0, sums, sums[::-1])
    sent = jnp.broadcast_to(sums[:, None], (2, row_count, 2, pair_count * 8))
    got = lax.all_to_all(
        sent.reshape(2 * row_count, 2, pair_count * 8), ("grp", "row"), 0, 0, tiled=True
    )
    got = jnp.sum(got.reshape(2, row_count, 2, pair_count, 4, 2), axis=1)
    got = got[0] + got[1][..., ::-1]
    got = got.transpose(1, 3, 0, 2).reshape(pair_count, 2, 8)
    chosen = place[:, None] == jnp.arange(8, dtype=jnp.int32)[None, :]
    ordered = jnp.sum(jnp.where(chosen, got[:, :, :, None], 0.0), axis=2)
    return ordered.reshape(pair_count, blocks) * scale


def solution(mesh):
    return jax.shard_map(
        on_device,
        mesh=mesh,
        in_specs=(
            P(BLOCK_AXES, "row", None, None),
            P(BLOCK_AXES, "row", None, None),
            P("row", None, None),
            P(BLOCK_AXES, None),
            P(),
        ),
        out_specs=P(BLOCK_AXES, None),
        check_vma=False,
    )
```

```python
import jax
import jax.numpy as jnp
from jax import lax
from jax.experimental import pallas as pl
from jax.experimental.pallas import tpu as pltpu
from jax.sharding import PartitionSpec as P

COULOMB = 0.4
LANES = 128
BLOCK_AXES = ("grp", "col")
VMEM_BYTES = 48 * 1024 * 1024


def cas_table(length):
    indices = jnp.arange(length, dtype=jnp.int32)
    products = indices[:, None] * indices[None, :] % length
    angles = products.astype(jnp.float32) * (2.0 * jnp.pi / length)
    return jnp.cos(angles) + jnp.sin(angles)


def signed_square(frequency, length):
    signed = ((frequency + length // 2) % length - length // 2).astype(jnp.float32)
    return signed * signed


def hartree(density):
    planes, length, depth = density.shape
    cas_rows = cas_table(length)
    highest = lax.Precision.HIGHEST
    grid_field = jnp.dot(density, cas_rows, precision=highest)
    grid_field = jnp.einsum("xyz,yv->xvz", grid_field, cas_rows, precision=highest)
    columns = lax.all_to_all(grid_field, "row", split_axis=1, concat_axis=0, tiled=True)
    columns = jnp.einsum("xyz,xu->uyz", columns, cas_rows, precision=highest)
    y_width = columns.shape[1]
    frequency = jnp.arange(length, dtype=jnp.int32)
    local_y = lax.axis_index("row") * y_width + jnp.arange(y_width, dtype=jnp.int32)
    squared_sum = (
        signed_square(frequency, length)[:, None, None]
        + signed_square(local_y, length)[None, :, None]
        + signed_square(frequency, length)[None, None, :]
    )
    kernel = jnp.where(squared_sum > 0, COULOMB / jnp.maximum(squared_sum, 1.0), 0.0)
    columns = jnp.einsum("xyz,xu->uyz", columns * kernel, cas_rows, precision=highest)
    grid_field = lax.all_to_all(columns, "row", split_axis=0, concat_axis=1, tiled=True)
    grid_field = jnp.einsum("xyz,yv->xvz", grid_field, cas_rows, precision=highest)
    grid_field = jnp.dot(grid_field, cas_rows, precision=highest)
    return grid_field * (1.0 / float(length) ** 3)


RING_Y, RING_X = 4, 2


def shift_col(value, dy, dx):
    pairs = [
        (y * RING_X + x, (y + dy) % RING_Y * RING_X + (x + dx) % RING_X)
        for y in range(RING_Y)
        for x in range(RING_X)
    ]
    return lax.ppermute(value, "col", pairs)


OFFSETS = ((0, 0), (1, 0), (3, 0), (0, 1), (2, 0), (1, 1), (3, 1), (2, 1))


def spread(piece):
    half = piece.shape[0] // 2
    from_below = shift_col(piece, 1, 0)
    from_above = shift_col(piece, -1, 0)
    from_side = shift_col(piece, 0, 1)
    far_low = shift_col(from_below[:half], 1, 0)
    far_high = shift_col(from_above[half:], -1, 0)
    side_below = shift_col(from_side, 1, 0)
    side_above = shift_col(from_side, -1, 0)
    far = jnp.concatenate([far_low, far_high], axis=0)
    side_far = shift_col(far, 0, 1)
    return [piece, from_below, from_above, from_side, far, side_below, side_above, side_far]


def swap_core(value):
    return lax.ppermute(value, "grp", [(0, 1), (1, 0)])


def pick_kernel(index_ref, held_ref, out_ref):
    rows = out_ref.shape[1]
    for block in range(out_ref.shape[0]):
        index = index_ref[block]
        start = pl.multiple_of(index % 2 * rows, rows)
        out_ref[block] = held_ref[index // 2, pl.ds(start, rows), :]


def pick(held, index, rows):
    return pl.pallas_call(
        pick_kernel,
        out_shape=jax.ShapeDtypeStruct((index.shape[0], rows, LANES), jnp.float32),
        in_specs=[
            pl.BlockSpec(memory_space=pltpu.SMEM),
            pl.BlockSpec(memory_space=pltpu.VMEM),
        ],
        out_specs=pl.BlockSpec(memory_space=pltpu.VMEM),
        compiler_params=pltpu.CompilerParams(vmem_limit_bytes=VMEM_BYTES),
        name="pick_occ",
    )(index, held)


PAIR_GROUP = 4


def add_products(total, first, densities, fields, rows):
    sums = [None] * (PAIR_GROUP * 8)
    for tile in range(rows // 8):
        cells = pl.ds(tile * 8, 8)
        right = [field[j, cells, :] for field in fields for j in range(2)]
        for k in range(PAIR_GROUP):
            left = densities(k, cells)
            for b in range(8):
                term = left * right[b]
                slot = k * 8 + b
                sums[slot] = term if sums[slot] is None else sums[slot] + term
    for slot, value in enumerate(sums):
        total[first * 8 + slot] += value


def start_total(total):
    @pl.when(pl.program_id(0) == 0)
    def _():
        total[...] = jnp.zeros_like(total)


def finish_total(total, out_ref):
    @pl.when(pl.program_id(0) == pl.num_programs(0) - 1)
    def _():
        lanes = jnp.sum(total[...], axis=1)
        out_ref[...] = lax.dot_general(
            jnp.ones((8, LANES), jnp.float32),
            lanes,
            (((1,), (1,)), ((), ())),
            precision=lax.Precision.HIGHEST,
            preferred_element_type=jnp.float32,
        )


def form_kernel(occ_index, vir_index, half, occ_ref, own_vir, mate_vir, *refs):
    fields, density_ref, out_ref, total = refs[:4], refs[4], refs[5], refs[6]
    rows = occ_ref.shape[2]
    per_block = own_vir.shape[0]
    start_total(total)
    for block, vir_ref in enumerate((own_vir.at[:, 0], mate_vir.at[:, 0])):

        @pl.loop(0, per_block // PAIR_GROUP)
        def _(group):
            first = block * per_block + group * PAIR_GROUP
            occ = [occ_index[first + k] for k in range(PAIR_GROUP)]
            vir = [vir_index[first + k] for k in range(PAIR_GROUP)]

            def density(k, cells):
                value = occ_ref[occ[k], 0, cells, :] * vir_ref[vir[k], cells, :]
                density_ref[first + k, cells, :] = value
                return value

            add_products(total, first, density, fields, rows)

    finish_total(total, out_ref)


def contract_kernel(density_ref, *refs):
    fields, out_ref, total = refs[:4], refs[4], refs[5]
    start_total(total)

    @pl.loop(0, density_ref.shape[0] // PAIR_GROUP)
    def _(group):
        first = group * PAIR_GROUP
        add_products(
            total,
            first,
            lambda k, cells: density_ref[first + k, cells, :],
            fields,
            density_ref.shape[1],
        )

    finish_total(total, out_ref)


TILE = 128


def form_and_contract(occ_index, vir_index, half, occ, own_vir, mate_vir, fields):
    pairs = occ_index.shape[0]
    orbitals, _, rows, _ = occ.shape
    per_block = own_vir.shape[0]
    return pl.pallas_call(
        form_kernel,
        grid_spec=pltpu.PrefetchScalarGridSpec(
            num_scalar_prefetch=3,
            grid=(rows // TILE,),
            in_specs=[
                pl.BlockSpec((orbitals, 1, TILE, LANES), lambda i, o, v, half: (0, half[0], i, 0)),
                pl.BlockSpec((per_block, 1, TILE, LANES), lambda i, o, v, half: (0, half[0], i, 0)),
                pl.BlockSpec((per_block, 1, TILE, LANES), lambda i, o, v, half: (0, 0, i, 0)),
            ]
            + [pl.BlockSpec((2, TILE, LANES), lambda i, o, v, half: (0, i, 0))] * 4,
            out_specs=[
                pl.BlockSpec((pairs, TILE, LANES), lambda i, o, v, half: (0, i, 0)),
                pl.BlockSpec((8, pairs * 8), lambda i, o, v, half: (0, 0)),
            ],
            scratch_shapes=[pltpu.VMEM((pairs * 8, 8, LANES), jnp.float32)],
        ),
        out_shape=[
            jax.ShapeDtypeStruct((pairs, rows, LANES), jnp.float32),
            jax.ShapeDtypeStruct((8, pairs * 8), jnp.float32),
        ],
        compiler_params=pltpu.CompilerParams(vmem_limit_bytes=VMEM_BYTES),
        cost_estimate=pl.CostEstimate(
            flops=17 * pairs * rows * LANES, bytes_accessed=26 * 1024 * 1024, transcendentals=0
        ),
        name="form_and_contract",
    )(occ_index, vir_index, half, occ, own_vir, mate_vir, *fields)


def contract(densities, fields):
    pairs, rows, _ = densities.shape
    return pl.pallas_call(
        contract_kernel,
        grid=(rows // TILE,),
        in_specs=[pl.BlockSpec((pairs, TILE, LANES), lambda i: (0, i, 0))]
        + [pl.BlockSpec((2, TILE, LANES), lambda i: (0, i, 0))] * 4,
        out_specs=pl.BlockSpec((8, pairs * 8), lambda i: (0, 0)),
        out_shape=jax.ShapeDtypeStruct((8, pairs * 8), jnp.float32),
        scratch_shapes=[pltpu.VMEM((pairs * 8, 8, LANES), jnp.float32)],
        compiler_params=pltpu.CompilerParams(vmem_limit_bytes=VMEM_BYTES),
        cost_estimate=pl.CostEstimate(
            flops=16 * pairs * rows * LANES, bytes_accessed=10 * 1024 * 1024, transcendentals=0
        ),
        name="contract",
    )(densities, *fields)


def on_device(occ_orbitals, vir_orbitals, xc_kernel, pairs, batch_slot):
    planes, size_y, size_z = xc_kernel.shape
    cell_count = planes * size_y * size_z
    row_count = lax.axis_size("row")
    scale = 1.0 / float(cell_count * row_count)
    grp = lax.axis_index("grp")
    col = lax.axis_index("col")
    blocks = lax.axis_size(BLOCK_AXES)
    block_index = grp * lax.axis_size("col") + col
    occ_local, vir_local = occ_orbitals.shape[0], vir_orbitals.shape[0]
    chunk_rows = cell_count // blocks // LANES
    half_rows = cell_count // 2 // LANES

    every_occ = lax.all_gather(occ_orbitals, BLOCK_AXES, axis=0, tiled=True)
    every_occ = every_occ.reshape(every_occ.shape[0], 2, half_rows, LANES)
    mate_pairs = swap_core(pairs)
    vir_halves = vir_orbitals.reshape(vir_local, 2, half_rows, LANES)
    mate_vir = swap_core(lax.dynamic_index_in_dim(vir_halves, 1 - grp, 1, keepdims=True))

    own_slot = jnp.take(batch_slot, block_index)
    own_pair = lax.dynamic_index_in_dim(pairs, own_slot, 0, keepdims=False)
    wanted = own_pair[0].astype(jnp.float32)
    chunks = occ_orbitals.reshape(occ_local, blocks, chunk_rows, LANES)
    chunks = chunks.transpose(1, 0, 2, 3).reshape(blocks, occ_local * chunk_rows, LANES)
    note = jnp.full((blocks, 8, LANES), wanted, jnp.float32)
    held = lax.all_to_all(
        jnp.concatenate([chunks, note], axis=1), BLOCK_AXES, 0, 0, tiled=True
    )
    wanted_all = held[:, occ_local * chunk_rows, 0].astype(jnp.int32)
    picked = pick(held, wanted_all, chunk_rows)
    own_occ = lax.all_to_all(picked, BLOCK_AXES, 0, 0, tiled=True)
    own_vir = lax.dynamic_index_in_dim(
        vir_orbitals, own_pair[1] - block_index * vir_local, 0, keepdims=False
    )
    sigma = own_occ.reshape(planes, size_y, size_z) * own_vir

    potential = hartree(sigma) + xc_kernel * sigma
    halves = potential.reshape(2, half_rows, LANES)
    kept = lax.dynamic_index_in_dim(halves, grp, 0, keepdims=True)
    moved = swap_core(lax.dynamic_index_in_dim(halves, 1 - grp, 0, keepdims=True))
    fields = spread(jnp.concatenate([kept, moved], axis=0))

    own_y, own_x = col // RING_X, col % RING_X
    places = [
        (own_y + RING_Y - dy) % RING_Y * RING_X + (own_x + RING_X - dx) % RING_X
        for dy, dx in OFFSETS
    ]
    place = jnp.stack(places).astype(jnp.int32)
    mate_block = (1 - grp) * lax.axis_size("col") + col
    densities, near = form_and_contract(
        jnp.concatenate([pairs[:, 0], mate_pairs[:, 0]]),
        jnp.concatenate(
            [pairs[:, 1] - block_index * vir_local, mate_pairs[:, 1] - mate_block * vir_local]
        ),
        jnp.full((1,), grp, jnp.int32),
        every_occ,
        vir_halves,
        mate_vir,
        fields[:4],
    )
    far = contract(densities, fields[4:])

    pair_count = pairs.shape[0]
    sums = jnp.stack([near[0], far[0]]).reshape(2, 2, pair_count * 8)
    sums = sums.transpose(1, 0, 2)
    sums = jnp.where(grp == 0, sums, sums[::-1])
    sent = jnp.broadcast_to(sums[:, None], (2, row_count, 2, pair_count * 8))
    got = lax.all_to_all(
        sent.reshape(2 * row_count, 2, pair_count * 8), ("grp", "row"), 0, 0, tiled=True
    )
    got = jnp.sum(got.reshape(2, row_count, 2, pair_count, 4, 2), axis=1)
    got = got[0] + got[1][..., ::-1]
    got = got.transpose(1, 3, 0, 2).reshape(pair_count, 2, 8)
    chosen = place[:, None] == jnp.arange(8, dtype=jnp.int32)[None, :]
    ordered = jnp.sum(jnp.where(chosen, got[:, :, :, None], 0.0), axis=2)
    return ordered.reshape(pair_count, blocks) * scale


def solution(mesh):
    return jax.shard_map(
        on_device,
        mesh=mesh,
        in_specs=(
            P(BLOCK_AXES, "row", None, None),
            P(BLOCK_AXES, "row", None, None),
            P("row", None, None),
            P(BLOCK_AXES, None),
            P(),
        ),
        out_specs=P(BLOCK_AXES, None),
        check_vma=False,
    )
```

```python
import jax
import jax.numpy as jnp
from jax import lax
from jax.experimental import pallas as pl
from jax.experimental.pallas import tpu as pltpu
from jax.sharding import PartitionSpec as P

COULOMB = 0.4
LANES = 128
BLOCK_AXES = ("grp", "col")
VMEM_BYTES = 48 * 1024 * 1024


def cas_table(length):
    indices = jnp.arange(length, dtype=jnp.int32)
    products = indices[:, None] * indices[None, :] % length
    angles = products.astype(jnp.float32) * (2.0 * jnp.pi / length)
    return jnp.cos(angles) + jnp.sin(angles)


def signed_square(frequency, length):
    signed = ((frequency + length // 2) % length - length // 2).astype(jnp.float32)
    return signed * signed


def planes_forward(density):
    cas_rows = cas_table(density.shape[1])
    highest = lax.Precision.HIGHEST
    grid_field = jnp.dot(density, cas_rows, precision=highest)
    return jnp.einsum("xyz,yv->xvz", grid_field, cas_rows, precision=highest)


def filter_columns(columns):
    length, y_width, _ = columns.shape
    cas_rows = cas_table(length)
    highest = lax.Precision.HIGHEST
    columns = jnp.einsum("xyz,xu->uyz", columns, cas_rows, precision=highest)
    frequency = jnp.arange(length, dtype=jnp.int32)
    local_y = lax.axis_index("row") * y_width + jnp.arange(y_width, dtype=jnp.int32)
    squared_sum = (
        signed_square(frequency, length)[:, None, None]
        + signed_square(local_y, length)[None, :, None]
        + signed_square(frequency, length)[None, None, :]
    )
    kernel = jnp.where(squared_sum > 0, COULOMB / jnp.maximum(squared_sum, 1.0), 0.0)
    return jnp.einsum("xyz,xu->uyz", columns * kernel, cas_rows, precision=highest)


def planes_back(grid_field):
    length = grid_field.shape[1]
    cas_rows = cas_table(length)
    highest = lax.Precision.HIGHEST
    grid_field = jnp.einsum("xyz,yv->xvz", grid_field, cas_rows, precision=highest)
    grid_field = jnp.dot(grid_field, cas_rows, precision=highest)
    return grid_field * (1.0 / float(length) ** 3)


RING_Y, RING_X = 4, 2


def shift_col(value, dy, dx):
    pairs = [
        (y * RING_X + x, (y + dy) % RING_Y * RING_X + (x + dx) % RING_X)
        for y in range(RING_Y)
        for x in range(RING_X)
    ]
    return lax.ppermute(value, "col", pairs)


OFFSETS = ((0, 0), (1, 0), (3, 0), (0, 1), (2, 0), (1, 1), (3, 1), (2, 1))


def spread(piece):
    low, high = piece[:1], piece[1:]
    from_side = shift_col(piece, 0, 1)
    below_low, above_high = shift_col(low, 1, 0), shift_col(high, -1, 0)
    below_high, above_low = shift_col(high, 1, 0), shift_col(low, -1, 0)
    far_low, far_high = shift_col(below_low, 1, 0), shift_col(above_high, -1, 0)
    side_below, side_above = shift_col(from_side, 1, 0), shift_col(from_side, -1, 0)
    last_low, last_high = shift_col(far_low, 0, 1), shift_col(far_high, 0, 1)
    near = [piece, below_low, below_high, above_low, above_high, from_side]
    return near, [far_low, far_high, side_below, side_above, last_low, last_high]


def swap_core(value):
    return lax.ppermute(value, "grp", [(0, 1), (1, 0)])


def pick_kernel(place_ref, *refs):
    arrays, out_ref, sems = refs[:-2], refs[-2], refs[-1]
    parts = [array.at[j] for array in arrays for j in range(array.shape[0])]
    for number in range(out_ref.shape[0]):
        for order, part in enumerate(parts):

            @pl.when(place_ref[number] == order)
            def _():
                pltpu.make_async_copy(part, out_ref.at[number], sems.at[number]).start()

    for number in range(out_ref.shape[0]):
        pltpu.make_async_copy(parts[0], out_ref.at[number], sems.at[number]).wait()


def pick(place, arrays):
    count = place.shape[0]
    return pl.pallas_call(
        pick_kernel,
        out_shape=jax.ShapeDtypeStruct((count,) + arrays[0].shape[1:], jnp.float32),
        in_specs=[pl.BlockSpec(memory_space=pltpu.SMEM)]
        + [pl.BlockSpec(memory_space=pl.ANY)] * len(arrays),
        out_specs=pl.BlockSpec(memory_space=pltpu.VMEM),
        scratch_shapes=[pltpu.SemaphoreType.DMA((count,))],
        compiler_params=pltpu.CompilerParams(vmem_limit_bytes=VMEM_BYTES),
        name="pick_occ",
    )(place, *arrays)


PAIR_GROUP = 4


def add_products(total, first, densities, fields, rows):
    sums = [None] * (PAIR_GROUP * 8)
    for tile in range(rows // 8):
        cells = pl.ds(tile * 8, 8)
        right = [field[j, cells, :] for field in fields for j in range(field.shape[0])]
        for k in range(PAIR_GROUP):
            left = densities(k, cells)
            for b in range(8):
                term = left * right[b]
                slot = k * 8 + b
                sums[slot] = term if sums[slot] is None else sums[slot] + term
    for slot, value in enumerate(sums):
        total[first * 8 + slot] += value


def start_total(total):
    @pl.when(pl.program_id(0) == 0)
    def _():
        total[...] = jnp.zeros_like(total)


def finish_total(total, out_ref):
    @pl.when(pl.program_id(0) == pl.num_programs(0) - 1)
    def _():
        lanes = jnp.sum(total[...], axis=1)
        out_ref[...] = lax.dot_general(
            jnp.ones((8, LANES), jnp.float32),
            lanes,
            (((1,), (1,)), ((), ())),
            precision=lax.Precision.HIGHEST,
            preferred_element_type=jnp.float32,
        )


def form_kernel(occ_index, vir_index, half, own_occ, mate_occ, own_vir, mate_vir, *refs):
    fields, (density_ref, out_ref, total) = refs[:-3], refs[-3:]
    held, rows, _ = own_occ.shape
    per_block = own_vir.shape[0]
    start_total(total)
    for block, vir_ref in enumerate((own_vir.at[:, 0], mate_vir.at[:, 0])):

        @pl.loop(0, per_block // PAIR_GROUP)
        def _(group):
            first = block * per_block + group * PAIR_GROUP
            occ = [occ_index[first + k] for k in range(PAIR_GROUP)]
            near = [index < held for index in occ]
            occ = [jnp.where(own, index, index - held) for own, index in zip(near, occ)]
            vir = [vir_index[first + k] for k in range(PAIR_GROUP)]

            def density(k, cells):
                left = jnp.where(near[k], own_occ[occ[k], cells, :], mate_occ[occ[k], cells, :])
                value = left * vir_ref[vir[k], cells, :]
                density_ref[first + k, cells, :] = value
                return value

            add_products(total, first, density, fields, rows)

    finish_total(total, out_ref)


def contract_kernel(density_ref, *refs):
    fields, (out_ref, total) = refs[:-2], refs[-2:]
    start_total(total)

    @pl.loop(0, density_ref.shape[0] // PAIR_GROUP)
    def _(group):
        first = group * PAIR_GROUP
        add_products(
            total,
            first,
            lambda k, cells: density_ref[first + k, cells, :],
            fields,
            density_ref.shape[1],
        )

    finish_total(total, out_ref)


TILE = 128


def form_and_contract(occ_index, vir_index, half, own_occ, mate_occ, own_vir, mate_vir, fields):
    pairs = occ_index.shape[0]
    held, rows, _ = own_occ.shape
    per_block = own_vir.shape[0]
    occ_spec = pl.BlockSpec((held, TILE, LANES), lambda i, o, v, half: (0, i, 0))
    return pl.pallas_call(
        form_kernel,
        grid_spec=pltpu.PrefetchScalarGridSpec(
            num_scalar_prefetch=3,
            grid=(rows // TILE,),
            in_specs=[
                occ_spec,
                occ_spec,
                pl.BlockSpec((per_block, 1, TILE, LANES), lambda i, o, v, half: (0, half[0], i, 0)),
                pl.BlockSpec((per_block, 1, TILE, LANES), lambda i, o, v, half: (0, 0, i, 0)),
            ]
            + [
                pl.BlockSpec((field.shape[0], TILE, LANES), lambda i, o, v, half: (0, i, 0))
                for field in fields
            ],
            out_specs=[
                pl.BlockSpec((pairs, TILE, LANES), lambda i, o, v, half: (0, i, 0)),
                pl.BlockSpec((8, pairs * 8), lambda i, o, v, half: (0, 0)),
            ],
            scratch_shapes=[pltpu.VMEM((pairs * 8, 8, LANES), jnp.float32)],
        ),
        out_shape=[
            jax.ShapeDtypeStruct((pairs, rows, LANES), jnp.float32),
            jax.ShapeDtypeStruct((8, pairs * 8), jnp.float32),
        ],
        compiler_params=pltpu.CompilerParams(vmem_limit_bytes=VMEM_BYTES),
        cost_estimate=pl.CostEstimate(
            flops=17 * pairs * rows * LANES, bytes_accessed=26 * 1024 * 1024, transcendentals=0
        ),
        name="form_and_contract",
    )(occ_index, vir_index, half, own_occ, mate_occ, own_vir, mate_vir, *fields)


def contract(densities, fields):
    pairs, rows, _ = densities.shape
    return pl.pallas_call(
        contract_kernel,
        grid=(rows // TILE,),
        in_specs=[pl.BlockSpec((pairs, TILE, LANES), lambda i: (0, i, 0))]
        + [pl.BlockSpec((field.shape[0], TILE, LANES), lambda i: (0, i, 0)) for field in fields],
        out_specs=pl.BlockSpec((8, pairs * 8), lambda i: (0, 0)),
        out_shape=jax.ShapeDtypeStruct((8, pairs * 8), jnp.float32),
        scratch_shapes=[pltpu.VMEM((pairs * 8, 8, LANES), jnp.float32)],
        compiler_params=pltpu.CompilerParams(vmem_limit_bytes=VMEM_BYTES),
        cost_estimate=pl.CostEstimate(
            flops=16 * pairs * rows * LANES, bytes_accessed=10 * 1024 * 1024, transcendentals=0
        ),
        name="contract",
    )(densities, *fields)


def on_device(occ_orbitals, vir_orbitals, xc_kernel, pairs, batch_slot):
    planes, size_y, size_z = xc_kernel.shape
    cell_count = planes * size_y * size_z
    row_count = lax.axis_size("row")
    scale = 1.0 / float(cell_count * row_count)
    grp = lax.axis_index("grp")
    col = lax.axis_index("col")
    blocks = lax.axis_size(BLOCK_AXES)
    block_index = grp * lax.axis_size("col") + col
    occ_local, vir_local = occ_orbitals.shape[0], vir_orbitals.shape[0]
    half_rows = cell_count // 2 // LANES
    own_y, own_x = col // RING_X, col % RING_X
    mate_block = (1 - grp) * lax.axis_size("col") + col
    places = [
        (own_y + RING_Y - dy) % RING_Y * RING_X + (own_x + RING_X - dx) % RING_X
        for dy, dx in OFFSETS
    ]
    place = jnp.stack(places).astype(jnp.int32)

    def order_of(col_index):
        same = col_index[:, None] == place[None, :]
        return jnp.sum(jnp.where(same, jnp.arange(8, dtype=jnp.int32), 0), axis=1)

    occ_near, occ_far = spread(occ_orbitals.reshape(occ_local, 2 * half_rows, LANES))
    occ_pieces = occ_near + occ_far
    mate_pairs = swap_core(pairs)
    vir_halves = vir_orbitals.reshape(vir_local, 2, half_rows, LANES)
    mate_vir = swap_core(lax.dynamic_index_in_dim(vir_halves, 1 - grp, 1, keepdims=True))

    own_pair = lax.dynamic_index_in_dim(pairs, batch_slot[block_index], 0, keepdims=False)
    mate_pair = lax.dynamic_index_in_dim(mate_pairs, batch_slot[mate_block], 0, keepdims=False)
    wanted = jnp.stack([own_pair[0], mate_pair[0]])
    wanted_place = order_of(wanted // occ_local % 8) * occ_local + wanted % occ_local
    picked = pick(wanted_place, occ_pieces)
    from_mate = swap_core(picked[1])
    own_occ = jnp.where(wanted[0] // occ_local // 8 == grp, picked[0], from_mate)
    own_vir = lax.dynamic_index_in_dim(
        vir_orbitals, own_pair[1] - block_index * vir_local, 0, keepdims=False
    )
    sigma = own_occ.reshape(planes, size_y, size_z) * own_vir
    columns = lax.all_to_all(
        planes_forward(sigma), "row", split_axis=1, concat_axis=0, tiled=True
    )
    field = lax.all_to_all(filter_columns(columns), "row", split_axis=0, concat_axis=1, tiled=True)
    potential = planes_back(field) + xc_kernel * sigma

    halves = potential.reshape(2, half_rows, LANES)
    kept = lax.dynamic_index_in_dim(halves, grp, 0, keepdims=True)
    moved = swap_core(lax.dynamic_index_in_dim(halves, 1 - grp, 0, keepdims=True))
    own_field = jnp.concatenate([kept, moved], axis=0)
    field_near, field_far = spread(own_field)

    def occ_half(half):
        parts = [
            lax.dynamic_slice_in_dim(part, half * half_rows, half_rows, 1) for part in occ_pieces
        ]
        return jnp.concatenate(parts, axis=0)

    own_occs, mate_occs = occ_half(grp), swap_core(occ_half(1 - grp))
    occ_index = jnp.concatenate([pairs[:, 0], mate_pairs[:, 0]])
    source = occ_index // occ_local
    occ_place = jnp.where(source // 8 == grp, 0, 8 * occ_local)
    occ_place = occ_place + order_of(source % 8) * occ_local + occ_index % occ_local
    densities, near = form_and_contract(
        occ_place,
        jnp.concatenate(
            [pairs[:, 1] - block_index * vir_local, mate_pairs[:, 1] - mate_block * vir_local]
        ),
        jnp.full((1,), grp, jnp.int32),
        own_occs,
        mate_occs,
        vir_halves,
        mate_vir,
        field_near,
    )
    far = contract(densities, field_far)

    pair_count = pairs.shape[0]
    sums = jnp.stack([near[0], far[0]]).reshape(2, 2, pair_count * 8)
    sums = sums.transpose(1, 0, 2)
    sums = jnp.where(grp == 0, sums, sums[::-1])
    sent = jnp.broadcast_to(sums[:, None], (2, row_count, 2, pair_count * 8))
    got = lax.all_to_all(
        sent.reshape(2 * row_count, 2, pair_count * 8), ("grp", "row"), 0, 0, tiled=True
    )
    got = jnp.sum(got.reshape(2, row_count, 2, pair_count, 4, 2), axis=1)
    got = got[0] + got[1][..., ::-1]
    got = got.transpose(1, 3, 0, 2).reshape(pair_count, 2, 8)
    chosen = place[:, None] == jnp.arange(8, dtype=jnp.int32)[None, :]
    ordered = jnp.sum(jnp.where(chosen, got[:, :, :, None], 0.0), axis=2)
    return ordered.reshape(pair_count, blocks) * scale


def solution(mesh):
    return jax.shard_map(
        on_device,
        mesh=mesh,
        in_specs=(
            P(BLOCK_AXES, "row", None, None),
            P(BLOCK_AXES, "row", None, None),
            P("row", None, None),
            P(BLOCK_AXES, None),
            P(),
        ),
        out_specs=P(BLOCK_AXES, None),
        check_vma=False,
    )
```

```python
import jax
import jax.numpy as jnp
import numpy as np
from jax import lax
from jax.experimental import pallas as pl
from jax.experimental.pallas import tpu as pltpu
from jax.sharding import PartitionSpec as P

COULOMB = 0.4
LANES = 128
BLOCK_AXES = ("grp", "col")
VMEM_BYTES = 48 * 1024 * 1024


def cas_table(length):
    indices = np.arange(length)
    angles = indices[:, None] * indices[None, :] % length * (2.0 * np.pi / length)
    return jnp.asarray((np.cos(angles) + np.sin(angles)).astype(np.float32))


def dot_exact(left, right):
    return jnp.dot(left, right, precision=lax.Precision.HIGHEST, preferred_element_type=jnp.float32)


def forward_kernel(flag_ref, vir_place, own_occ, mate_occ, vir_ref, cas_ref, sigma_ref, out_ref):
    planes, length, _ = sigma_ref.shape
    cas = cas_ref[...]
    left = jnp.where(flag_ref[0] != 0, own_occ[...], mate_occ[...])
    sigma = left.reshape(sigma_ref.shape) * vir_ref[0]
    sigma_ref[...] = sigma
    field = dot_exact(sigma.reshape(planes * length, length), cas).reshape(sigma.shape)
    field = jnp.stack([dot_exact(cas, field[x]) for x in range(planes)])
    out_ref[...] = jnp.swapaxes(field, 0, 1)


def forward(flag, vir_place, own_occ, mate_occ, vir, cas):
    _, planes, length, _ = vir.shape
    whole = pl.BlockSpec(memory_space=pltpu.VMEM)
    return pl.pallas_call(
        forward_kernel,
        grid_spec=pltpu.PrefetchScalarGridSpec(
            num_scalar_prefetch=2,
            grid=(1,),
            in_specs=[
                whole,
                whole,
                pl.BlockSpec((1, planes, length, length), lambda i, f, v: (v[0], 0, 0, 0)),
                whole,
            ],
            out_specs=[whole, whole],
        ),
        out_shape=[
            jax.ShapeDtypeStruct((planes, length, length), jnp.float32),
            jax.ShapeDtypeStruct((length, planes, length), jnp.float32),
        ],
        compiler_params=pltpu.CompilerParams(vmem_limit_bytes=VMEM_BYTES),
        name="forward",
    )(flag, vir_place, own_occ, mate_occ, vir, cas)


def filter_kernel(first_ref, in_ref, cas_ref, out_ref):
    blocks, width, part, length = in_ref.shape
    cas = cas_ref[...]

    def square(index):
        signed = jnp.where(index >= length // 2, index - length, index)
        return (signed * signed).astype(jnp.float32)

    side = square(lax.broadcasted_iota(jnp.int32, (length, length), 0))
    side = side + square(lax.broadcasted_iota(jnp.int32, (length, length), 1))
    for v in range(width):
        column = dot_exact(cas, in_ref[:, v].reshape(length, length))
        squared_sum = side + square(first_ref[0] + v + jnp.zeros((1, length), jnp.int32))
        factor = jnp.where(squared_sum > 0, COULOMB / jnp.maximum(squared_sum, 1.0), 0.0)
        out_ref[:, v] = dot_exact(cas, column * factor).reshape(blocks, part, length)


def filter_columns(first, columns, cas):
    return pl.pallas_call(
        filter_kernel,
        out_shape=jax.ShapeDtypeStruct(columns.shape, jnp.float32),
        in_specs=[pl.BlockSpec(memory_space=pltpu.SMEM)]
        + [pl.BlockSpec(memory_space=pltpu.VMEM)] * 2,
        out_specs=pl.BlockSpec(memory_space=pltpu.VMEM),
        compiler_params=pltpu.CompilerParams(vmem_limit_bytes=VMEM_BYTES),
        name="filter_columns",
    )(first, columns, cas)


def back_kernel(half_ref, in_ref, sigma_ref, xc_ref, cas_ref, kept_ref, given_ref, held):
    length, planes, _ = in_ref.shape
    cas = cas_ref[...]
    field = dot_exact(in_ref[...].reshape(length * planes, length), cas)
    held[...] = jnp.swapaxes(field.reshape(length, planes, length), 0, 1)
    scale = 1.0 / float(length) ** 3
    for half, out_ref in ((half_ref[0], kept_ref), (1 - half_ref[0], given_ref)):
        for number in range(planes // 2):
            x = half * (planes // 2) + number
            value = dot_exact(cas, held[x]) * scale + xc_ref[x] * sigma_ref[x]
            out_ref[0, number * length : (number + 1) * length, :] = value


def back(half, field, sigma, xc_kernel, cas):
    length, planes, _ = field.shape
    shape = jax.ShapeDtypeStruct((1, planes // 2 * length, length), jnp.float32)
    return pl.pallas_call(
        back_kernel,
        out_shape=[shape, shape],
        in_specs=[pl.BlockSpec(memory_space=pltpu.SMEM)]
        + [pl.BlockSpec(memory_space=pltpu.VMEM)] * 4,
        out_specs=[pl.BlockSpec(memory_space=pltpu.VMEM)] * 2,
        scratch_shapes=[pltpu.VMEM((planes, length, length), jnp.float32)],
        compiler_params=pltpu.CompilerParams(vmem_limit_bytes=VMEM_BYTES),
        name="back",
    )(half, field, sigma, xc_kernel, cas)


RING_Y, RING_X = 4, 2


def shift_col(value, dy, dx):
    pairs = [
        (y * RING_X + x, (y + dy) % RING_Y * RING_X + (x + dx) % RING_X)
        for y in range(RING_Y)
        for x in range(RING_X)
    ]
    return lax.ppermute(value, "col", pairs)


OFFSETS = ((0, 0), (1, 0), (3, 0), (0, 1), (2, 0), (1, 1), (3, 1), (2, 1))


def spread(piece, *others):
    from_below, from_above = shift_col(piece, 1, 0), shift_col(piece, -1, 0)
    from_side = shift_col(piece, 0, 1)
    from_side, from_below, from_above, others = lax.optimization_barrier(
        (from_side, from_below, from_above, others)
    )
    far = [shift_col(from_below[:1], 1, 0), shift_col(from_above[1:], -1, 0)]
    far = jnp.concatenate(far, axis=0)
    side_below, side_above = shift_col(from_side, 1, 0), shift_col(from_side, -1, 0)
    near = [piece, from_below, from_above, from_side]
    return near, [far, side_below, side_above, shift_col(far, 0, 1)], others


def swap_core(value):
    return lax.ppermute(value, "grp", [(0, 1), (1, 0)])


def pick_kernel(place_ref, *refs):
    arrays, out_ref, sems = refs[:-2], refs[-2], refs[-1]
    parts = [array.at[j] for array in arrays for j in range(array.shape[0])]
    for number in range(out_ref.shape[0]):
        for order, part in enumerate(parts):

            @pl.when(place_ref[number] == order)
            def _():
                pltpu.make_async_copy(part, out_ref.at[number], sems.at[number]).start()

    for number in range(out_ref.shape[0]):
        pltpu.make_async_copy(parts[0], out_ref.at[number], sems.at[number]).wait()


def pick(place, arrays):
    count = place.shape[0]
    return pl.pallas_call(
        pick_kernel,
        out_shape=jax.ShapeDtypeStruct((count,) + arrays[0].shape[1:], jnp.float32),
        in_specs=[pl.BlockSpec(memory_space=pltpu.SMEM)]
        + [pl.BlockSpec(memory_space=pl.ANY)] * len(arrays),
        out_specs=pl.BlockSpec(memory_space=pltpu.VMEM),
        scratch_shapes=[pltpu.SemaphoreType.DMA((count,))],
        compiler_params=pltpu.CompilerParams(vmem_limit_bytes=VMEM_BYTES),
        name="pick_occ",
    )(place, *arrays)


PAIR_GROUP = 4


def add_products(total, first, densities, fields, rows):
    count = sum(field.shape[0] for field in fields)
    sums = [None] * (PAIR_GROUP * count)
    for tile in range(rows // 8):
        cells = pl.ds(tile * 8, 8)
        right = [field[j, cells, :] for field in fields for j in range(field.shape[0])]
        for k in range(PAIR_GROUP):
            left = densities(k, cells)
            for b in range(count):
                term = left * right[b]
                slot = k * count + b
                sums[slot] = term if sums[slot] is None else sums[slot] + term
    for slot, value in enumerate(sums):
        total[first * count + slot] += value


def start_total(total):
    @pl.when(pl.program_id(0) == 0)
    def _():
        total[...] = jnp.zeros_like(total)


def finish_total(total, out_ref):
    @pl.when(pl.program_id(0) == pl.num_programs(0) - 1)
    def _():
        lanes = jnp.sum(total[...], axis=1)
        out_ref[...] = lax.dot_general(
            jnp.ones((8, LANES), jnp.float32),
            lanes,
            (((1,), (1,)), ((), ())),
            precision=lax.Precision.HIGHEST,
            preferred_element_type=jnp.float32,
        )


def form_kernel(occ_index, vir_index, half, own_occ, mate_occ, own_vir, mate_vir, density_ref):
    held, rows, _ = own_occ.shape
    per_block = own_vir.shape[0]
    for block, vir_ref in enumerate((own_vir.at[:, 0], mate_vir.at[:, 0])):

        @pl.loop(block * per_block, (block + 1) * per_block)
        def _(pair):
            index, vir = occ_index[pair], vir_index[pair]

            @pl.when(index < held)
            def _():
                density_ref[0, pair] = own_occ[index] * vir_ref[vir]

            @pl.when(index >= held)
            def _():
                density_ref[0, pair] = mate_occ[index - held] * vir_ref[vir]


def contract_kernel(density_ref, *refs):
    fields, (out_ref, total) = refs[:-2], refs[-2:]
    start_total(total)

    @pl.loop(0, density_ref.shape[1] // PAIR_GROUP)
    def _(group):
        first = group * PAIR_GROUP
        add_products(
            total,
            first,
            lambda k, cells: density_ref[0, first + k, cells, :],
            fields,
            density_ref.shape[2],
        )

    finish_total(total, out_ref)


TILE = 128


def form_densities(occ_index, vir_index, half, own_occ, mate_occ, own_vir, mate_vir):
    pairs = occ_index.shape[0]
    held, rows, _ = own_occ.shape
    per_block = own_vir.shape[0]
    occ_spec = pl.BlockSpec((held, TILE, LANES), lambda i, o, v, half: (0, i, 0))
    return pl.pallas_call(
        form_kernel,
        grid_spec=pltpu.PrefetchScalarGridSpec(
            num_scalar_prefetch=3,
            grid=(rows // TILE,),
            in_specs=[
                occ_spec,
                occ_spec,
                pl.BlockSpec((per_block, 1, TILE, LANES), lambda i, o, v, half: (0, half[0], i, 0)),
                pl.BlockSpec((per_block, 1, TILE, LANES), lambda i, o, v, half: (0, half[0], i, 0)),
            ],
            out_specs=pl.BlockSpec((1, pairs, TILE, LANES), lambda i, o, v, half: (i, 0, 0, 0)),
        ),
        out_shape=jax.ShapeDtypeStruct((rows // TILE, pairs, TILE, LANES), jnp.float32),
        compiler_params=pltpu.CompilerParams(vmem_limit_bytes=VMEM_BYTES),
        cost_estimate=pl.CostEstimate(
            flops=pairs * rows * LANES, bytes_accessed=24 * 1024 * 1024, transcendentals=0
        ),
        name="form_densities",
    )(occ_index, vir_index, half, own_occ, mate_occ, own_vir, mate_vir)


def contract(densities, fields):
    tiles, pairs, rows, _ = densities.shape
    count = sum(field.shape[0] for field in fields)
    return pl.pallas_call(
        contract_kernel,
        grid=(tiles,),
        in_specs=[pl.BlockSpec((1, pairs, rows, LANES), lambda i: (i, 0, 0, 0))]
        + [pl.BlockSpec((field.shape[0], rows, LANES), lambda i: (0, i, 0)) for field in fields],
        out_specs=pl.BlockSpec((8, pairs * count), lambda i: (0, 0)),
        out_shape=jax.ShapeDtypeStruct((8, pairs * count), jnp.float32),
        scratch_shapes=[pltpu.VMEM((pairs * count, 8, LANES), jnp.float32)],
        compiler_params=pltpu.CompilerParams(vmem_limit_bytes=VMEM_BYTES),
        cost_estimate=pl.CostEstimate(
            flops=2 * count * tiles * pairs * rows * LANES, bytes_accessed=10 * 1024 * 1024, transcendentals=0
        ),
        name="contract",
    )(densities, *fields)


def on_device(occ_orbitals, vir_orbitals, xc_kernel, pairs, batch_slot):
    planes, size_y, size_z = xc_kernel.shape
    cell_count = planes * size_y * size_z
    row_count = lax.axis_size("row")
    scale = 1.0 / float(cell_count * row_count)
    grp = lax.axis_index("grp")
    col = lax.axis_index("col")
    blocks = lax.axis_size(BLOCK_AXES)
    block_index = grp * lax.axis_size("col") + col
    occ_local, vir_local = occ_orbitals.shape[0], vir_orbitals.shape[0]
    half_rows = cell_count // 2 // LANES
    own_y, own_x = col // RING_X, col % RING_X
    mate_block = (1 - grp) * lax.axis_size("col") + col
    places = [
        (own_y + RING_Y - dy) % RING_Y * RING_X + (own_x + RING_X - dx) % RING_X
        for dy, dx in OFFSETS
    ]
    place = jnp.stack(places).astype(jnp.int32)

    def order_of(col_index):
        same = col_index[:, None] == place[None, :]
        return jnp.sum(jnp.where(same, jnp.arange(8, dtype=jnp.int32), 0), axis=1)

    mate_pairs = swap_core(pairs)
    vir_halves = vir_orbitals.reshape(vir_local, 2, half_rows, LANES)
    mate_vir = swap_core(vir_halves)

    own_pair = lax.dynamic_index_in_dim(pairs, batch_slot[block_index], 0, keepdims=False)
    mate_pair = lax.dynamic_index_in_dim(mate_pairs, batch_slot[mate_block], 0, keepdims=False)
    wanted = jnp.stack([own_pair[0], mate_pair[0]])
    wanted_place = order_of(wanted // occ_local % 8) * occ_local + wanted % occ_local
    own_vir_place = (own_pair[1] - block_index * vir_local).reshape(1)
    occ_index = jnp.concatenate([pairs[:, 0], mate_pairs[:, 0]])
    source = occ_index // occ_local
    occ_place = jnp.where(source // 8 == grp, 0, 8 * occ_local)
    occ_place = occ_place + order_of(source % 8) * occ_local + occ_index % occ_local
    vir_place = jnp.concatenate(
        [pairs[:, 1] - block_index * vir_local, mate_pairs[:, 1] - mate_block * vir_local]
    )

    occ_near, occ_far, (wanted_place, occ_place, vir_place) = spread(
        occ_orbitals.reshape(occ_local, 2 * half_rows, LANES), wanted_place, occ_place, vir_place
    )
    occ_pieces = occ_near + occ_far
    picked = pick(wanted_place, occ_pieces)
    from_mate = swap_core(picked[1])
    cas = cas_table(size_z)
    as_flag = jnp.where(wanted[0] // occ_local // 8 == grp, 1, 0).reshape(1)
    sigma, field = forward(as_flag, own_vir_place, picked[0], from_mate, vir_orbitals, cas)
    columns = lax.all_to_all(field, "row", split_axis=0, concat_axis=0, tiled=True)
    columns = columns.reshape(row_count, -1, planes, size_z)
    first = (lax.axis_index("row") * (size_y // row_count)).reshape(1)
    columns = filter_columns(first, columns, cas)
    columns, *occ_pieces[7:] = lax.optimization_barrier((columns, *occ_pieces[7:]))

    def occ_half(half):
        parts = [
            lax.dynamic_slice_in_dim(part, half * half_rows, half_rows, 1) for part in occ_pieces
        ]
        return jnp.concatenate(parts, axis=0)

    mate_occs, own_occs = swap_core(occ_half(1 - grp)), occ_half(grp)
    densities = form_densities(
        occ_place, vir_place, jnp.full((1,), grp, jnp.int32), own_occs, mate_occs, vir_halves, mate_vir
    )
    field = lax.all_to_all(columns, "row", split_axis=0, concat_axis=0, tiled=True)
    half = jnp.full((1,), grp, jnp.int32)
    kept, given = back(half, field.reshape(size_y, planes, size_z), sigma, xc_kernel, cas)
    own_field = jnp.concatenate([kept, swap_core(given)], axis=0)
    field_near, field_far, (densities,) = spread(own_field, densities)

    near = contract(densities, field_near + field_far[:1])
    far = contract(densities, field_far[1:])

    pair_count = pairs.shape[0]
    sums = [part[0].reshape(2, pair_count, -1) for part in (near, far)]
    sums = jnp.concatenate(sums, axis=2)
    sums = jnp.where(grp == 0, sums, sums[::-1])
    sent = jnp.broadcast_to(sums[:, None], (2, row_count, pair_count, blocks))
    got = lax.all_to_all(
        sent.reshape(2 * row_count, 2, pair_count * blocks // 2), ("grp", "row"), 0, 0, tiled=True
    )
    got = jnp.sum(got.reshape(2, row_count, pair_count, 8, 2), axis=1)
    got = got[0] + got[1][..., ::-1]
    got = got.transpose(0, 2, 1)
    chosen = place[:, None] == jnp.arange(8, dtype=jnp.int32)[None, :]
    ordered = jnp.sum(jnp.where(chosen, got[:, :, :, None], 0.0), axis=2)
    return ordered.reshape(pair_count, blocks) * scale


def solution(mesh):
    return jax.shard_map(
        on_device,
        mesh=mesh,
        in_specs=(
            P(BLOCK_AXES, "row", None, None),
            P(BLOCK_AXES, "row", None, None),
            P("row", None, None),
            P(BLOCK_AXES, None),
            P(),
        ),
        out_specs=P(BLOCK_AXES, None),
        check_vma=False,
    )
```

```python
import jax
import jax.numpy as jnp
import numpy as np
from jax import lax
from jax.experimental import pallas as pl
from jax.experimental.pallas import tpu as pltpu
from jax.sharding import PartitionSpec as P

COULOMB = 0.4
LANES = 128
BLOCK_AXES = ("grp", "col")
VMEM_BYTES = 48 * 1024 * 1024


def cas_table(length):
    indices = np.arange(length)
    angles = indices[:, None] * indices[None, :] % length * (2.0 * np.pi / length)
    return jnp.asarray((np.cos(angles) + np.sin(angles)).astype(np.float32))


def dot_exact(left, right):
    return jnp.dot(left, right, precision=lax.Precision.HIGHEST, preferred_element_type=jnp.float32)


def forward_kernel(flag_ref, vir_place, own_occ, mate_occ, vir_ref, cas_ref, sigma_ref, out_ref):
    planes, length, _ = sigma_ref.shape
    cas = cas_ref[...]
    left = jnp.where(flag_ref[0] != 0, own_occ[...], mate_occ[...])
    sigma = left.reshape(sigma_ref.shape) * vir_ref[0]
    sigma_ref[...] = sigma
    field = dot_exact(sigma.reshape(planes * length, length), cas).reshape(sigma.shape)
    field = jnp.stack([dot_exact(cas, field[x]) for x in range(planes)])
    out_ref[...] = jnp.swapaxes(field, 0, 1)


def forward(flag, vir_place, own_occ, mate_occ, vir, cas):
    _, planes, length, _ = vir.shape
    whole = pl.BlockSpec(memory_space=pltpu.VMEM)
    return pl.pallas_call(
        forward_kernel,
        grid_spec=pltpu.PrefetchScalarGridSpec(
            num_scalar_prefetch=2,
            grid=(1,),
            in_specs=[
                whole,
                whole,
                pl.BlockSpec((1, planes, length, length), lambda i, f, v: (v[0], 0, 0, 0)),
                whole,
            ],
            out_specs=[whole, whole],
        ),
        out_shape=[
            jax.ShapeDtypeStruct((planes, length, length), jnp.float32),
            jax.ShapeDtypeStruct((length, planes, length), jnp.float32),
        ],
        compiler_params=pltpu.CompilerParams(vmem_limit_bytes=VMEM_BYTES),
        name="forward",
    )(flag, vir_place, own_occ, mate_occ, vir, cas)


def filter_kernel(first_ref, in_ref, cas_ref, out_ref):
    blocks, width, part, length = in_ref.shape
    cas = cas_ref[...]

    def square(index):
        signed = jnp.where(index >= length // 2, index - length, index)
        return (signed * signed).astype(jnp.float32)

    side = square(lax.broadcasted_iota(jnp.int32, (length, length), 0))
    side = side + square(lax.broadcasted_iota(jnp.int32, (length, length), 1))
    for v in range(width):
        column = dot_exact(cas, in_ref[:, v].reshape(length, length))
        squared_sum = side + square(first_ref[0] + v + jnp.zeros((1, length), jnp.int32))
        factor = jnp.where(squared_sum > 0, COULOMB / jnp.maximum(squared_sum, 1.0), 0.0)
        out_ref[:, v] = dot_exact(cas, column * factor).reshape(blocks, part, length)


def filter_columns(first, columns, cas):
    return pl.pallas_call(
        filter_kernel,
        out_shape=jax.ShapeDtypeStruct(columns.shape, jnp.float32),
        in_specs=[pl.BlockSpec(memory_space=pltpu.SMEM)]
        + [pl.BlockSpec(memory_space=pltpu.VMEM)] * 2,
        out_specs=pl.BlockSpec(memory_space=pltpu.VMEM),
        compiler_params=pltpu.CompilerParams(vmem_limit_bytes=VMEM_BYTES),
        name="filter_columns",
    )(first, columns, cas)


def back_kernel(half_ref, in_ref, sigma_ref, xc_ref, cas_ref, kept_ref, given_ref, held):
    length, planes, _ = in_ref.shape
    cas = cas_ref[...]
    field = dot_exact(in_ref[...].reshape(length * planes, length), cas)
    held[...] = jnp.swapaxes(field.reshape(length, planes, length), 0, 1)
    scale = 1.0 / float(length) ** 3
    for half, out_ref in ((half_ref[0], kept_ref), (1 - half_ref[0], given_ref)):
        for number in range(planes // 2):
            x = half * (planes // 2) + number
            value = dot_exact(cas, held[x]) * scale + xc_ref[x] * sigma_ref[x]
            out_ref[0, number * length : (number + 1) * length, :] = value


def back(half, field, sigma, xc_kernel, cas):
    length, planes, _ = field.shape
    shape = jax.ShapeDtypeStruct((1, planes // 2 * length, length), jnp.float32)
    return pl.pallas_call(
        back_kernel,
        out_shape=[shape, shape],
        in_specs=[pl.BlockSpec(memory_space=pltpu.SMEM)]
        + [pl.BlockSpec(memory_space=pltpu.VMEM)] * 4,
        out_specs=[pl.BlockSpec(memory_space=pltpu.VMEM)] * 2,
        scratch_shapes=[pltpu.VMEM((planes, length, length), jnp.float32)],
        compiler_params=pltpu.CompilerParams(vmem_limit_bytes=VMEM_BYTES),
        name="back",
    )(half, field, sigma, xc_kernel, cas)


RING_Y, RING_X = 4, 2


def shift_col(value, dy, dx):
    pairs = [
        (y * RING_X + x, (y + dy) % RING_Y * RING_X + (x + dx) % RING_X)
        for y in range(RING_Y)
        for x in range(RING_X)
    ]
    return lax.ppermute(value, "col", pairs)


OFFSETS = ((0, 0), (1, 0), (3, 0), (0, 1), (2, 0), (1, 1), (3, 1), (2, 1))


def spread(piece, *others):
    from_below, from_above = shift_col(piece, 1, 0), shift_col(piece, -1, 0)
    from_side = shift_col(piece, 0, 1)
    from_side, from_below, from_above, others = lax.optimization_barrier(
        (from_side, from_below, from_above, others)
    )
    far = [shift_col(from_below[:1], 1, 0), shift_col(from_above[1:], -1, 0)]
    far = jnp.concatenate(far, axis=0)
    side_below, side_above = shift_col(from_side, 1, 0), shift_col(from_side, -1, 0)
    near = [piece, from_below, from_above, from_side]
    return near, [far, side_below, side_above, shift_col(far, 0, 1)], others


def swap_core(value):
    return lax.ppermute(value, "grp", [(0, 1), (1, 0)])


def pick_kernel(place_ref, *refs):
    arrays, outs, sems = refs[:-3], refs[-3:-1], refs[-1]
    parts = [array.at[j] for array in arrays for j in range(array.shape[0])]
    for number, out_ref in enumerate(outs):
        for order, part in enumerate(parts):

            @pl.when(place_ref[number] == order)
            def _():
                pltpu.make_async_copy(part, out_ref, sems.at[number]).start()

    for number, out_ref in enumerate(outs):
        pltpu.make_async_copy(parts[0], out_ref, sems.at[number]).wait()


def pick(place, arrays):
    shape = jax.ShapeDtypeStruct(arrays[0].shape[1:], jnp.float32)
    return pl.pallas_call(
        pick_kernel,
        out_shape=[shape, shape],
        in_specs=[pl.BlockSpec(memory_space=pltpu.SMEM)]
        + [pl.BlockSpec(memory_space=pl.ANY)] * len(arrays),
        out_specs=[pl.BlockSpec(memory_space=pltpu.VMEM)] * 2,
        scratch_shapes=[pltpu.SemaphoreType.DMA((2,))],
        compiler_params=pltpu.CompilerParams(vmem_limit_bytes=VMEM_BYTES),
        name="pick_occ",
    )(place, *arrays)


PAIR_GROUP = 4


def add_products(total, first, densities, fields, rows):
    count = sum(field.shape[0] for field in fields)
    sums = [None] * (PAIR_GROUP * count)
    for tile in range(rows // 8):
        cells = pl.ds(tile * 8, 8)
        right = [field[j, cells, :] for field in fields for j in range(field.shape[0])]
        for k in range(PAIR_GROUP):
            left = densities(k, cells)
            for b in range(count):
                term = left * right[b]
                slot = k * count + b
                sums[slot] = term if sums[slot] is None else sums[slot] + term
    for slot, value in enumerate(sums):
        total[first * count + slot] += value


def start_total(total):
    @pl.when(pl.program_id(0) == 0)
    def _():
        total[...] = jnp.zeros_like(total)


def finish_total(total, out_ref):
    @pl.when(pl.program_id(0) == pl.num_programs(0) - 1)
    def _():
        lanes = jnp.sum(total[...], axis=1)
        out_ref[...] = lax.dot_general(
            jnp.ones((8, LANES), jnp.float32),
            lanes,
            (((1,), (1,)), ((), ())),
            precision=lax.Precision.HIGHEST,
            preferred_element_type=jnp.float32,
        )


def form_kernel(occ_index, vir_index, half, own_occ, mate_occ, own_vir, mate_vir, density_ref):
    held, rows, _ = own_occ.shape
    per_block = own_vir.shape[0]
    for block, vir_ref in enumerate((own_vir.at[:, 0], mate_vir.at[:, 0])):

        @pl.loop(block * per_block, (block + 1) * per_block)
        def _(pair):
            index, vir = occ_index[pair], vir_index[pair]

            @pl.when(index < held)
            def _():
                density_ref[0, pair] = own_occ[index] * vir_ref[vir]

            @pl.when(index >= held)
            def _():
                density_ref[0, pair] = mate_occ[index - held] * vir_ref[vir]


def contract_kernel(density_ref, *refs):
    fields, (out_ref, total) = refs[:-2], refs[-2:]
    start_total(total)

    @pl.loop(0, density_ref.shape[1] // PAIR_GROUP)
    def _(group):
        first = group * PAIR_GROUP
        add_products(
            total,
            first,
            lambda k, cells: density_ref[0, first + k, cells, :],
            fields,
            density_ref.shape[2],
        )

    finish_total(total, out_ref)


TILE = 128


def form_densities(occ_index, vir_index, half, own_occ, mate_occ, own_vir, mate_vir):
    pairs = occ_index.shape[0]
    held, rows, _ = own_occ.shape
    per_block = own_vir.shape[0]
    occ_spec = pl.BlockSpec((held, TILE, LANES), lambda i, o, v, half: (0, i, 0))
    return pl.pallas_call(
        form_kernel,
        grid_spec=pltpu.PrefetchScalarGridSpec(
            num_scalar_prefetch=3,
            grid=(rows // TILE,),
            in_specs=[
                occ_spec,
                occ_spec,
                pl.BlockSpec((per_block, 1, TILE, LANES), lambda i, o, v, half: (0, half[0], i, 0)),
                pl.BlockSpec((per_block, 1, TILE, LANES), lambda i, o, v, half: (0, half[0], i, 0)),
            ],
            out_specs=pl.BlockSpec((1, pairs, TILE, LANES), lambda i, o, v, half: (i, 0, 0, 0)),
        ),
        out_shape=jax.ShapeDtypeStruct((rows // TILE, pairs, TILE, LANES), jnp.float32),
        compiler_params=pltpu.CompilerParams(vmem_limit_bytes=VMEM_BYTES),
        cost_estimate=pl.CostEstimate(
            flops=pairs * rows * LANES, bytes_accessed=24 * 1024 * 1024, transcendentals=0
        ),
        name="form_densities",
    )(occ_index, vir_index, half, own_occ, mate_occ, own_vir, mate_vir)


def contract(densities, fields):
    tiles, pairs, rows, _ = densities.shape
    count = sum(field.shape[0] for field in fields)
    return pl.pallas_call(
        contract_kernel,
        grid=(tiles,),
        in_specs=[pl.BlockSpec((1, pairs, rows, LANES), lambda i: (i, 0, 0, 0))]
        + [pl.BlockSpec((field.shape[0], rows, LANES), lambda i: (0, i, 0)) for field in fields],
        out_specs=pl.BlockSpec((8, pairs * count), lambda i: (0, 0)),
        out_shape=jax.ShapeDtypeStruct((8, pairs * count), jnp.float32),
        scratch_shapes=[pltpu.VMEM((pairs * count, 8, LANES), jnp.float32)],
        compiler_params=pltpu.CompilerParams(vmem_limit_bytes=VMEM_BYTES),
        cost_estimate=pl.CostEstimate(
            flops=2 * count * tiles * pairs * rows * LANES, bytes_accessed=10 * 1024 * 1024, transcendentals=0
        ),
        name="contract",
    )(densities, *fields)


def on_device(occ_orbitals, vir_orbitals, xc_kernel, pairs, batch_slot):
    planes, size_y, size_z = xc_kernel.shape
    cell_count = planes * size_y * size_z
    row_count = lax.axis_size("row")
    scale = 1.0 / float(cell_count * row_count)
    grp = lax.axis_index("grp")
    col = lax.axis_index("col")
    blocks = lax.axis_size(BLOCK_AXES)
    block_index = grp * lax.axis_size("col") + col
    occ_local, vir_local = occ_orbitals.shape[0], vir_orbitals.shape[0]
    half_rows = cell_count // 2 // LANES
    own_y, own_x = col // RING_X, col % RING_X
    mate_block = (1 - grp) * lax.axis_size("col") + col
    places = [
        (own_y + RING_Y - dy) % RING_Y * RING_X + (own_x + RING_X - dx) % RING_X
        for dy, dx in OFFSETS
    ]
    place = jnp.stack(places).astype(jnp.int32)

    def order_of(col_index):
        same = col_index[:, None] == place[None, :]
        return jnp.sum(jnp.where(same, jnp.arange(8, dtype=jnp.int32), 0), axis=1)

    mate_pairs = swap_core(pairs)
    vir_halves = vir_orbitals.reshape(vir_local, 2, half_rows, LANES)
    mate_vir = swap_core(vir_halves)

    own_pair = lax.dynamic_index_in_dim(pairs, batch_slot[block_index], 0, keepdims=False)
    mate_pair = lax.dynamic_index_in_dim(mate_pairs, batch_slot[mate_block], 0, keepdims=False)
    wanted = jnp.stack([own_pair[0], mate_pair[0]])
    wanted_place = order_of(wanted // occ_local % 8) * occ_local + wanted % occ_local
    own_vir_place = (own_pair[1] - block_index * vir_local).reshape(1)
    occ_index = jnp.concatenate([pairs[:, 0], mate_pairs[:, 0]])
    source = occ_index // occ_local
    occ_place = jnp.where(source // 8 == grp, 0, 8 * occ_local)
    occ_place = occ_place + order_of(source % 8) * occ_local + occ_index % occ_local
    vir_place = jnp.concatenate(
        [pairs[:, 1] - block_index * vir_local, mate_pairs[:, 1] - mate_block * vir_local]
    )

    occ_near, occ_far, (wanted_place, occ_place, vir_place) = spread(
        occ_orbitals.reshape(occ_local, 2 * half_rows, LANES), wanted_place, occ_place, vir_place
    )
    occ_pieces = occ_near + occ_far
    picked = pick(wanted_place, occ_pieces)
    from_mate = swap_core(picked[1])
    cas = cas_table(size_z)
    as_flag = jnp.where(wanted[0] // occ_local // 8 == grp, 1, 0).reshape(1)
    sigma, field = forward(as_flag, own_vir_place, picked[0], from_mate, vir_orbitals, cas)
    columns = lax.all_to_all(field, "row", split_axis=0, concat_axis=0, tiled=True)
    columns = columns.reshape(row_count, -1, planes, size_z)
    first = (lax.axis_index("row") * (size_y // row_count)).reshape(1)
    columns = filter_columns(first, columns, cas)
    columns, *occ_pieces[7:] = lax.optimization_barrier((columns, *occ_pieces[7:]))

    def occ_half(half):
        parts = [
            lax.dynamic_slice_in_dim(part, half * half_rows, half_rows, 1) for part in occ_pieces
        ]
        return jnp.concatenate(parts, axis=0)

    mate_occs, own_occs = swap_core(occ_half(1 - grp)), occ_half(grp)
    densities = form_densities(
        occ_place, vir_place, jnp.full((1,), grp, jnp.int32), own_occs, mate_occs, vir_halves, mate_vir
    )
    field = lax.all_to_all(columns, "row", split_axis=0, concat_axis=0, tiled=True)
    half = jnp.full((1,), grp, jnp.int32)
    kept, given = back(half, field.reshape(size_y, planes, size_z), sigma, xc_kernel, cas)
    own_field = jnp.concatenate([kept, swap_core(given)], axis=0)
    field_near, field_far, (densities,) = spread(own_field, densities)

    near = contract(densities, field_near + field_far[:1])
    far = contract(densities, field_far[1:])

    pair_count = pairs.shape[0]
    sums = [part[0].reshape(2, pair_count, -1) for part in (near, far)]
    sums = jnp.concatenate(sums, axis=2)
    sums = jnp.where(grp == 0, sums, sums[::-1])
    sent = jnp.broadcast_to(sums[:, None], (2, row_count, pair_count, blocks))
    got = lax.all_to_all(
        sent.reshape(2 * row_count, 2, pair_count * blocks // 2), ("grp", "row"), 0, 0, tiled=True
    )
    got = jnp.sum(got.reshape(2, row_count, pair_count, 8, 2), axis=1)
    got = got[0] + got[1][..., ::-1]
    got = got.transpose(0, 2, 1)
    chosen = place[:, None] == jnp.arange(8, dtype=jnp.int32)[None, :]
    ordered = jnp.sum(jnp.where(chosen, got[:, :, :, None], 0.0), axis=2)
    return ordered.reshape(pair_count, blocks) * scale


def solution(mesh):
    return jax.shard_map(
        on_device,
        mesh=mesh,
        in_specs=(
            P(BLOCK_AXES, "row", None, None),
            P(BLOCK_AXES, "row", None, None),
            P("row", None, None),
            P(BLOCK_AXES, None),
            P(),
        ),
        out_specs=P(BLOCK_AXES, None),
        check_vma=False,
    )
```
